32 devices in a mesh: rows: 4 (over y, x), cols: 8 (over z, core).
Axes of the slice: x: 2, y: 2, z: 4, core: 2. Of those that a mesh axis runs over, the one named last changes fastest.
Arguments:
- forget_grad: bfloat16 [4096, 4096], P('rows', 'cols'), may hold values from -6 to 6
- left_basis: bfloat16 [4096, 4096], P('rows', 'cols'), may hold values from -0.09375 to 0.09375
- right_basis: bfloat16 [4096, 4096], P('rows', 'cols'), may hold values from -0.09375 to 0.09375
- first_moment: float32 [4096, 4096], P('rows', 'cols'), may hold values from -6 to 6
- second_moment: float32 [4096, 4096], P('rows', 'cols'), may hold values from 0.05 to 2
Outputs:
- step_dir: bfloat16 [4096, 4096], P('rows', 'cols')
- new_first: float32 [4096, 4096], P('rows', 'cols')
- new_second: float32 [4096, 4096], P('rows', 'cols')
The draws below stay inside these ranges and needn't reach their ends.
All inputs are finite; a program needn't handle non-finite values.
Results may differ from the reference program's by a relative error of at most 0.019.
Values may be sent and summed in bfloat16 or wider, within the bound.
No kernel may reach another device: no remote copies, remote signals or barrier semaphores. Data moves between devices by JAX's collectives and lax.ppermute only.
A program may use at most 64 MiB of HBM per device.

```python
import math
import jax
import jax.numpy as jnp
from jax import lax

D = 4096
N_ROWS = 4
N_COLS = 8


def block_scale(rng, shape, pieces, low, largest):
    level = 1.0
    for position, parts in pieces:
        draws = jax.random.uniform(jax.random.fold_in(jax.random.fold_in(rng, 6), position), (parts,), jnp.float32, low / len(pieces), largest / len(pieces))
        level = level * jnp.repeat(jnp.exp(draws), shape[position] // parts).reshape((-1,) + (1,) * (len(shape) - 1 - position))
    return level


def gaussian(own_key, extent, scale, limit, shards=(), kind=jnp.bfloat16):
    drawn = scale * jax.random.normal(own_key, extent, jnp.float32)
    if shards:
        drawn = drawn * block_scale(own_key, extent, shards, -0.22, 0.18)
    return jnp.clip(drawn, -limit, limit).astype(kind)


def setup_inputs(seed: int = 0) -> dict:
    streams_of = jax.random.split(jax.random.key(seed), 6)
    return {
        "forget_grad": gaussian(streams_of[0], (D, D), 1.0, 6.0, ((0, 4), (1, 8))),
        "left_basis": gaussian(streams_of[1], (D, D), D ** -0.5, 0.09375, ((0, 4), (1, 8))),
        "right_basis": gaussian(streams_of[2], (D, D), D ** -0.5, 0.09375, ((0, 4), (1, 8))),
        "first_moment": gaussian(streams_of[3], (D, D), 1.0, 6.0, ((0, 4), (1, 8)), jnp.float32),
        "second_moment": jnp.clip(jnp.exp(math.log(2.0) - 3.6888794 * jax.random.uniform(streams_of[4], (D, D), jnp.float32) ** block_scale(streams_of[4], (D, D), ((0, 4), (1, 8)), -0.2, 0.2)), 0.05, 2.0),
    }


beta_first = 0.9
beta_second = 0.95
corr_first = 1.0 - 0.9 ** 10
corr_second = 1.0 - 0.95 ** 10
epsilon = 1e-08

def rounded(value):
    low = lax.optimization_barrier(value.astype(jnp.bfloat16))
    return low.astype(jnp.float32)

def reference(forget_grad, left_basis, right_basis, first_moment, second_moment):
    negated = -forget_grad
    half_rotated = jnp.dot(negated, right_basis, preferred_element_type=jnp.float32).astype(jnp.bfloat16)
    row_block = D // N_ROWS

    def rotate_block(accum, index):
        first_row = (index * row_block).astype(jnp.int32)
        half_part = lax.dynamic_slice_in_dim(half_rotated, first_row, row_block, 0)
        left_part = lax.dynamic_slice_in_dim(left_basis, first_row, row_block, 0)
        term = lax.dot_general(half_part, left_part, (((0,), (0,)), ((), ())), preferred_element_type=jnp.float32)
        return (accum + rounded(term), None)
    rotated, _ = lax.scan(rotate_block, jnp.zeros((D, D), jnp.float32), jnp.arange(N_ROWS, dtype=jnp.int32))
    new_first = beta_first * first_moment + (1.0 - beta_first) * rotated
    new_second = beta_second * second_moment + (1.0 - beta_second) * rotated * rotated
    normalized = (new_first / corr_first / (jnp.sqrt(new_second / corr_second) + epsilon)).astype(jnp.bfloat16)
    back_half = jnp.dot(right_basis, normalized, preferred_element_type=jnp.float32).astype(jnp.bfloat16)
    col_block = D // N_COLS

    def step_block(accum, index):
        first_col = (index * col_block).astype(jnp.int32)
        back_part = lax.dynamic_slice_in_dim(back_half, first_col, col_block, 1)
        left_part = lax.dynamic_slice_in_dim(left_basis, first_col, col_block, 1)
        term = lax.dot_general(back_part, left_part, (((1,), (1,)), ((), ())), preferred_element_type=jnp.float32)
        return (accum + rounded(term), None)
    step_trans, _ = lax.scan(step_block, jnp.zeros((D, D), jnp.float32), jnp.arange(N_COLS, dtype=jnp.int32))
    step_dir = step_trans.T.astype(jnp.bfloat16)
    return (step_dir, new_first, new_second)
```

```python
import jax
import jax.numpy as jnp
from jax import lax
from jax.sharding import PartitionSpec as P

beta_first = 0.9
beta_second = 0.95
corr_first = 1.0 - 0.9**10
corr_second = 1.0 - 0.95**10
epsilon = 1e-08

bf16 = jnp.bfloat16
f32 = jnp.float32


def bits_of(count, reverse):
    bits = list(range(count.bit_length() - 1))
    return bits[::-1] if reverse else bits


def swap(block, count, bit):
    return lax.ppermute(block, "rows", [(i, i ^ (1 << bit)) for i in range(count)])


def my_bit(bit):
    return (lax.axis_index("rows") >> bit) & 1


def scatter_sum(parts, reverse):
    count = parts.shape[0]
    held = list(range(count.bit_length() - 1))[::-1]
    parts = parts.reshape((2,) * len(held) + parts.shape[1:])
    for bit in bits_of(count, reverse):
        axis = held.index(bit)
        mine = my_bit(bit)
        got = swap(lax.dynamic_index_in_dim(parts, 1 - mine, axis, False), count, bit)
        kept = lax.dynamic_index_in_dim(parts, mine, axis, False)
        held.remove(bit)
        total = kept.astype(f32) + got.astype(f32)
        parts = total.astype(bf16) if held else total
    return parts


def gather(block, count, reverse):
    rest = block.shape
    held = []
    for bit in bits_of(count, reverse):
        got = swap(block, count, bit)
        mine = my_bit(bit)
        axis = sum(other > bit for other in held)
        block = jnp.where(mine == 0, jnp.stack([block, got], axis), jnp.stack([got, block], axis))
        held.append(bit)
    return block.reshape((count,) + rest)


def make_local(rows, cols):
    def local(forget_grad, left_basis, right_basis, first_moment, second_moment):
        width = right_basis.shape[1]
        depth = right_basis.shape[0]
        per = cols // rows
        sub = width // rows

        grad_rows = lax.all_gather(forget_grad, "cols", axis=1, tiled=True)

        dealt = lax.all_to_all(right_basis.reshape(per, rows, sub, width), "rows", 1, 0)
        dealt = dealt.reshape(depth, width)
        cuts = [0, width * 3 // 4, width]
        spans = list(zip(cuts[:-1], cuts[1:]))
        right_rows = [
            lax.all_gather(dealt[:, lo:hi], "cols", axis=1, tiled=True) for lo, hi in spans
        ]
        left_rows = lax.all_gather(left_basis, "cols", axis=1, tiled=True)

        half = lax.dot_general(
            grad_rows, left_basis, (((0,), (0,)), ((), ())), preferred_element_type=f32
        ).astype(bf16)
        half = half.reshape(cols, rows, sub, width).swapaxes(0, 1)
        cut = cols // 2
        half = jnp.concatenate(
            [scatter_sum(half[:, :cut], False), scatter_sum(half[:, cut:], True)], 0
        ).astype(bf16).reshape(depth, width)

        first = first_moment.reshape(per, width, width)
        second = second_moment.reshape(per, width, width)
        back = None
        rotated = []
        cut = per // 2
        for (lo, hi), basis in zip(spans, right_rows):
            parts = lax.dot_general(
                basis, half, (((0,), (0,)), ((), ())), preferred_element_type=f32
            ).astype(bf16)
            parts = parts.reshape(rows, per, hi - lo, width)
            normals = []
            pair = []
            for reverse, own in ((False, slice(0, cut)), (True, slice(cut, per))):
                turned = -scatter_sum(parts[:, own], reverse)
                pair.append(turned)
                new_first = beta_first * first[own, lo:hi] + (1.0 - beta_first) * turned
                new_second = beta_second * second[own, lo:hi] + (1.0 - beta_second) * turned * turned
                normal = new_first / corr_first / (jnp.sqrt(new_second / corr_second) + epsilon)
                normals.append(gather(normal.astype(bf16), rows, reverse))
            rotated.append(jnp.concatenate(pair, 0))
            normals = jnp.concatenate(normals, 1).reshape(cols * (hi - lo), width)
            term = jnp.dot(basis, normals, preferred_element_type=f32)
            back = term if back is None else back + term
        rotated = jnp.concatenate(rotated, 1).reshape(depth, width)
        new_first = beta_first * first_moment + (1.0 - beta_first) * rotated
        new_second = beta_second * second_moment + (1.0 - beta_second) * rotated * rotated

        back = back.astype(bf16).reshape(cols, sub, width)
        back = lax.all_to_all(back, "cols", 0, 1).reshape(sub, cols * width)
        cut = sub // 2
        back = jnp.concatenate([gather(back[:cut], rows, False), gather(back[cut:], rows, True)], 1)
        back = back.reshape(width, cols * width)
        step_dir = lax.dot_general(
            left_rows, back, (((1,), (1,)), ((), ())), preferred_element_type=f32
        ).astype(bf16)
        return (step_dir, new_first, new_second)

    return local


def solution(mesh):
    spec = P("rows", "cols")
    return jax.shard_map(
        make_local(mesh.shape["rows"], mesh.shape["cols"]),
        mesh=mesh,
        in_specs=(spec,) * 5,
        out_specs=(spec,) * 3,
        check_vma=False,
    )
```

```python
import jax
import jax.numpy as jnp
from jax import lax
from jax.experimental.layout import Layout, with_layout_constraint
from jax.sharding import PartitionSpec as P

beta_first = 0.9
beta_second = 0.95
corr_first = 1.0 - 0.9**10
corr_second = 1.0 - 0.95**10
epsilon = 1e-08

bf16 = jnp.bfloat16
f32 = jnp.float32
chunks = 2


def rows_first(value):
    return with_layout_constraint(value, Layout(major_to_minor=tuple(range(value.ndim))))


def swap(block, count, mask):
    return lax.ppermute(block, "rows", [(i, i ^ mask) for i in range(count)])


def partners(count):
    return sorted(range(1, count), key=lambda mask: -mask.bit_count())


def scatter_sum(parts, axis):
    count = parts.shape[axis]
    me = lax.axis_index("rows")
    got = [
        swap(lax.dynamic_index_in_dim(parts, me ^ mask, axis, False), count, mask)
        for mask in partners(count)
    ]
    total = lax.dynamic_index_in_dim(parts, me, axis, False).astype(f32)
    for term in got:
        total = total + term.astype(f32)
    return total


def gather(block, count):
    me = lax.axis_index("rows")
    got = [(mask, swap(block, count, mask)) for mask in partners(count)]
    whole = lax.dynamic_update_index_in_dim(
        jnp.zeros((count,) + block.shape, block.dtype), block, me, 0
    )
    for mask, term in got:
        whole = lax.dynamic_update_index_in_dim(whole, term, me ^ mask, 0)
    return whole


def deal(parts):
    count = parts.shape[1]
    me = lax.axis_index("rows")
    own = lax.dynamic_index_in_dim(parts, me, 1, False)
    whole = lax.dynamic_update_index_in_dim(jnp.zeros((count,) + own.shape, own.dtype), own, me, 0)
    got = [
        (mask, swap(lax.dynamic_index_in_dim(parts, me ^ mask, 1, False), count, mask))
        for mask in partners(count)
    ]
    for mask, term in got:
        whole = lax.dynamic_update_index_in_dim(whole, term, me ^ mask, 0)
    return whole


def rotate_left(grad, left, later, rows, cols):
    depth, width = grad.shape
    sub = width // rows
    half = cols // 4
    index = lax.axis_index("cols")
    core, odd, pair = index & 1, (index >> 1) & 1, index >> 2
    left_other = lax.ppermute(left, "cols", [(i, i ^ 2) for i in range(cols)])
    moved = []
    for step in range(half):
        route = []
        for chip in range(half):
            for odd_chip in range(2):
                source, target = odd_chip * half + chip, 2 * ((chip + step) % half) + odd_chip
                route += [(2 * source + c, 2 * target + c) for c in range(2)]
        if moved:
            grad, moved[-1], left_other, later = lax.optimization_barrier(
                (grad, moved[-1], left_other, later)
            )
        moved.append(lax.ppermute(grad, "cols", route))
    moved[-1], later, left = lax.optimization_barrier((moved[-1], later, left))
    left_pair = jnp.concatenate([left_other, left], 1)
    whole = jnp.zeros((2, half, 2, sub, width), bf16)
    for step, block in enumerate(moved):
        other = lax.ppermute(block, "cols", [(i, i ^ 1) for i in range(cols)])
        both = jnp.where(core == 0, jnp.stack([block, other]), jnp.stack([other, block]))
        parts = lax.dot_general(
            both, left_pair, (((1,), (0,)), ((), ())), preferred_element_type=f32
        ).astype(bf16)
        parts = scatter_sum(parts.reshape(2, rows, sub, 2 * width), 1).astype(bf16)
        got = lax.ppermute(parts[..., :width], "cols", [(i, i ^ 2) for i in range(cols)])
        chip = lax.rem(pair + half - step, half)
        for half_index, value in ((odd, parts[..., width:]), (1 - odd, got)):
            whole = lax.dynamic_update_slice(
                whole, value[None, None], (half_index, chip, 0, 0, 0)
            )
    return whole.reshape(depth, width), later, left


def make_local(rows, cols):
    def local(forget_grad, left_basis, right_basis, first_moment, second_moment):
        depth, width = right_basis.shape
        per = cols // rows
        sub = width // rows
        mid = width // 2
        spans = (slice(0, mid), slice(mid, width))

        dealt = deal(right_basis.reshape(per, rows, sub, width)).reshape(depth, width)
        half, dealt, left = rotate_left(forget_grad, left_basis, dealt, rows, cols)
        basis = [lax.all_gather(dealt[:, span], "cols", axis=1, tiled=True) for span in spans]
        left_rows = lax.all_gather(left, "cols", axis=1, tiled=True)

        first = first_moment.reshape(per, 2, mid, width)
        second = second_moment.reshape(per, 2, mid, width)

        def turn(c, span):
            parts = lax.dot_general(
                basis[c], half[:, span], (((0,), (0,)), ((), ())), preferred_element_type=f32
            ).astype(bf16)
            return -scatter_sum(rows_first(parts).reshape(rows, per, mid, -1), 0)

        def normalize(c, span, value):
            new_first = beta_first * first[:, c, :, span] + (1.0 - beta_first) * value
            new_second = beta_second * second[:, c, :, span] + (1.0 - beta_second) * value * value
            normal = new_first / corr_first / (jnp.sqrt(new_second / corr_second) + epsilon)
            return gather(normal.astype(bf16), rows).reshape(cols * mid, -1)

        value = turn(0, slice(0, width))
        back = jnp.dot(basis[0], normalize(0, slice(0, width), value), preferred_element_type=f32)
        values = [turn(1, span) for span in spans]
        rotated = jnp.stack([value, jnp.concatenate(values, 2)], 1).reshape(depth, width)

        step_dir = None
        left_rows = left_rows.reshape(depth, cols, 2, mid)
        for c, span in enumerate(spans):
            normals = normalize(1, span, values[c])
            term = jnp.dot(basis[1], normals, preferred_element_type=f32) + back[:, span]
            term = rows_first(term.astype(bf16)).reshape(cols, sub, mid)
            term = lax.all_to_all(term, "cols", 0, 1).reshape(sub, cols * mid)
            term = lax.dot_general(
                left_rows[:, :, c].reshape(depth, cols * mid),
                gather(term, rows).reshape(width, cols * mid),
                (((1,), (1,)), ((), ())),
                preferred_element_type=f32,
            )
            step_dir = term if step_dir is None else step_dir + term
        step_dir = step_dir.astype(bf16)

        new_first = beta_first * first_moment + (1.0 - beta_first) * rotated
        new_second = beta_second * second_moment + (1.0 - beta_second) * rotated * rotated
        return (step_dir, new_first, new_second)

    return local


def solution(mesh):
    spec = P("rows", "cols")
    return jax.shard_map(
        make_local(mesh.shape["rows"], mesh.shape["cols"]),
        mesh=mesh,
        in_specs=(spec,) * 5,
        out_specs=(spec,) * 3,
        check_vma=False,
    )
```

```python
import jax
import jax.numpy as jnp
from jax import lax
from jax.experimental.layout import Layout, with_layout_constraint
from jax.sharding import PartitionSpec as P

beta_first = 0.9
beta_second = 0.95
corr_first = 1.0 - 0.9**10
corr_second = 1.0 - 0.95**10
epsilon = 1e-08

bf16 = jnp.bfloat16
f32 = jnp.float32
chunks = 2


def rows_first(value):
    return with_layout_constraint(value, Layout(major_to_minor=tuple(range(value.ndim))))


def swap(block, count, mask):
    return lax.ppermute(block, "rows", [(i, i ^ mask) for i in range(count)])


def partners(count):
    return sorted(range(1, count), key=lambda mask: -mask.bit_count())


def scatter_sum(parts, axis):
    count = parts.shape[axis]
    me = lax.axis_index("rows")
    got = [
        swap(lax.dynamic_index_in_dim(parts, me ^ mask, axis, False), count, mask)
        for mask in partners(count)
    ]
    total = lax.dynamic_index_in_dim(parts, me, axis, False).astype(f32)
    for term in got:
        total = total + term.astype(f32)
    return total, got[0]


def gather(block, count, before=None):
    me = lax.axis_index("rows")
    got = [(mask, swap(block, count, mask)) for mask in partners(count)]
    if before is not None:
        block, _ = lax.optimization_barrier((block, before))
    whole = lax.dynamic_update_index_in_dim(
        jnp.zeros((count,) + block.shape, block.dtype), block, me, 0
    )
    for mask, term in got:
        whole = lax.dynamic_update_index_in_dim(whole, term, me ^ mask, 0)
    return whole


def deal(parts):
    count = parts.shape[1]
    me = lax.axis_index("rows")
    own = lax.dynamic_index_in_dim(parts, me, 1, False)
    whole = lax.dynamic_update_index_in_dim(jnp.zeros((count,) + own.shape, own.dtype), own, me, 0)
    got = [
        (mask, swap(lax.dynamic_index_in_dim(parts, me ^ mask, 1, False), count, mask))
        for mask in partners(count)
    ]
    for mask, term in got:
        whole = lax.dynamic_update_index_in_dim(whole, term, me ^ mask, 0)
    return whole


def product(blocks, left):
    return lax.dot_general(
        blocks, left, (((1,), (0,)), ((), ())), preferred_element_type=f32
    ).astype(bf16)


def rotate_left(grad, left, later, rows, cols):
    depth, width = grad.shape
    sub = width // rows
    half = cols // 4
    index = lax.axis_index("cols")
    core, odd, pair = index & 1, (index >> 1) & 1, index >> 2
    left_pair = jnp.concatenate(
        [lax.ppermute(left, "cols", [(i, i ^ 2) for i in range(cols)]), left], 1
    )
    def along(step, value):
        route = []
        for chip in range(half):
            for odd_chip in range(2):
                source, target = odd_chip * half + chip, 2 * ((chip + step) % half) + odd_chip
                route += [(2 * source + c, 2 * target + c) for c in range(2)]
        return lax.ppermute(value, "cols", route)

    whole = jnp.zeros((2, half, 2, sub, width), bf16)
    block = along(0, grad)
    for step in range(half):
        if step < half - 1:
            grad, block, left_pair, later = lax.optimization_barrier((grad, block, left_pair, later))
            ahead = along(step + 1, grad)
        other = lax.ppermute(block, "cols", [(i, i ^ 1) for i in range(cols)])
        both = jnp.where(core == 0, jnp.stack([block, other]), jnp.stack([other, block]))
        parts = product(both, left_pair).reshape(2, rows, sub, 2 * width)
        mark = parts
        sums, got = scatter_sum(parts, 1)
        sums = sums.astype(bf16)
        if step == half - 2:
            later, _, _ = lax.optimization_barrier((later, ahead, got))
        if step < half - 1:
            block, _ = lax.optimization_barrier((ahead, sums))
        got = lax.ppermute(sums[..., :width], "cols", [(i, i ^ 2) for i in range(cols)])
        chip = lax.rem(pair + half - step, half)
        for half_index, value in ((odd, sums[..., width:]), (1 - odd, got)):
            whole = lax.dynamic_update_slice(
                whole, value[None, None], (half_index, chip, 0, 0, 0)
            )
    return whole.reshape(depth, width), later, mark


def make_local(rows, cols):
    def local(forget_grad, left_basis, right_basis, first_moment, second_moment):
        depth, width = right_basis.shape
        per = cols // rows
        sub = width // rows
        mid = width // 2
        spans = (slice(0, mid), slice(mid, width))

        dealt = deal(right_basis.reshape(per, rows, sub, width)).reshape(depth, width)
        half, dealt, mark = rotate_left(forget_grad, left_basis, dealt, rows, cols)
        late, left, _ = lax.optimization_barrier((dealt[:, mid:], left_basis, mark))
        basis = [lax.all_gather(x, "cols", axis=1, tiled=True) for x in (dealt[:, :mid], late)]
        left_rows = lax.all_gather(left, "cols", axis=1, tiled=True)

        first = first_moment.reshape(per, 2, mid, width)
        second = second_moment.reshape(per, 2, mid, width)

        def turn(c, span):
            parts = lax.dot_general(
                basis[c], half[:, span], (((0,), (0,)), ((), ())), preferred_element_type=f32
            ).astype(bf16)
            return -scatter_sum(rows_first(parts).reshape(rows, per, mid, -1), 0)[0]

        def normalize(c, span, value):
            new_first = beta_first * first[:, c, :, span] + (1.0 - beta_first) * value
            new_second = beta_second * second[:, c, :, span] + (1.0 - beta_second) * value * value
            normal = new_first / corr_first / (jnp.sqrt(new_second / corr_second) + epsilon)
            return gather(normal.astype(bf16), rows).reshape(cols * mid, -1)

        value = turn(0, slice(0, width))
        back = jnp.dot(basis[0], normalize(0, slice(0, width), value), preferred_element_type=f32)
        values = [turn(1, span) for span in spans]
        rotated = jnp.stack([value, jnp.concatenate(values, 2)], 1).reshape(depth, width)

        step_dir = None
        left_rows = left_rows.reshape(depth, cols, 2, mid)
        term = back
        for c, span in enumerate(spans):
            normals, _ = lax.optimization_barrier((normalize(1, span, values[c]), term))
            term = jnp.dot(basis[1], normals, preferred_element_type=f32) + back[:, span]
            term = rows_first(term.astype(bf16)).reshape(cols, sub, mid)
            full = lax.all_to_all(term, "cols", 0, 1).reshape(sub, cols * mid)
            full = lax.dot_general(
                left_rows[:, :, c].reshape(depth, cols * mid),
                gather(full, rows, step_dir).reshape(width, cols * mid),
                (((1,), (1,)), ((), ())),
                preferred_element_type=f32,
            )
            step_dir = full if step_dir is None else step_dir + full
        step_dir = step_dir.astype(bf16)

        new_first = beta_first * first_moment + (1.0 - beta_first) * rotated
        new_second = beta_second * second_moment + (1.0 - beta_second) * rotated * rotated
        return (step_dir, new_first, new_second)

    return local


def solution(mesh):
    spec = P("rows", "cols")
    return jax.shard_map(
        make_local(mesh.shape["rows"], mesh.shape["cols"]),
        mesh=mesh,
        in_specs=(spec,) * 5,
        out_specs=(spec,) * 3,
        check_vma=False,
    )
```

```python
import jax
import jax.numpy as jnp
from jax import lax
from jax.experimental.layout import Layout, with_layout_constraint
from jax.sharding import PartitionSpec as P

beta_first = 0.9
beta_second = 0.95
corr_first = 1.0 - 0.9**10
corr_second = 1.0 - 0.95**10
epsilon = 1e-08

bf16 = jnp.bfloat16
f32 = jnp.float32
chunks = 2


def rows_first(value):
    return with_layout_constraint(value, Layout(major_to_minor=tuple(range(value.ndim))))


def swap(block, count, mask):
    return lax.ppermute(block, "rows", [(i, i ^ mask) for i in range(count)])


def partners(count):
    return sorted(range(1, count), key=lambda mask: -mask.bit_count())


def halve(parts, reverse):
    count = parts.shape[0]
    me = lax.axis_index("rows")
    bits = list(range(count.bit_length() - 1))
    held = bits[::-1]
    parts = parts.reshape((2,) * len(held) + parts.shape[1:])
    for bit in bits[::-1] if reverse else bits:
        axis = held.index(bit)
        mine = (me >> bit) & 1
        got = swap(lax.dynamic_index_in_dim(parts, 1 - mine, axis, False), count, 1 << bit)
        kept = lax.dynamic_index_in_dim(parts, mine, axis, False)
        held.remove(bit)
        total = kept.astype(f32) + got.astype(f32)
        parts = total.astype(bf16) if held else total
    return parts


def scatter_sum(parts):
    cut = parts.shape[1] // 2
    return jnp.concatenate([halve(parts[:, :cut], False), halve(parts[:, cut:], True)], 0)


def gather(block, count, before=None):
    me = lax.axis_index("rows")
    held = {0: block}
    bits = [1 << b for b in range(count.bit_length() - 1)]
    for bit in bits[:-2]:
        held.update({mask ^ bit: swap(held[mask], count, bit) for mask in list(held)})
    low, high = bits[-2:]
    near = {m ^ b: swap(held[m], count, b) for b in (low, high) for m in list(held)}
    cut = block.shape[0] // 2
    far = {
        m ^ low ^ high: jnp.concatenate(
            [swap(near[m ^ low][:cut], count, high), swap(near[m ^ high][cut:], count, low)], 0
        )
        for m in held
    }
    if before is not None:
        block, _ = lax.optimization_barrier((block, before))
    whole = jnp.zeros((count,) + block.shape, block.dtype)
    for mask, term in {**held, **near, **far, 0: block}.items():
        whole = lax.dynamic_update_index_in_dim(whole, term, me ^ mask, 0)
    return whole


def deal(parts):
    count = parts.shape[1]
    me = lax.axis_index("rows")
    own = lax.dynamic_index_in_dim(parts, me, 1, False)
    whole = lax.dynamic_update_index_in_dim(jnp.zeros((count,) + own.shape, own.dtype), own, me, 0)
    got = [
        (mask, swap(lax.dynamic_index_in_dim(parts, me ^ mask, 1, False), count, mask))
        for mask in partners(count)
    ]
    for mask, term in got:
        whole = lax.dynamic_update_index_in_dim(whole, term, me ^ mask, 0)
    return whole


def product(blocks, left):
    return lax.dot_general(
        blocks, left, (((1,), (0,)), ((), ())), preferred_element_type=f32
    ).astype(bf16)


def rotate_left(grad, left, later, rows, cols):
    depth, width = grad.shape
    sub = width // rows
    half = cols // 4
    index = lax.axis_index("cols")
    core, odd, pair = index & 1, (index >> 1) & 1, index >> 2
    left_pair = jnp.concatenate(
        [lax.ppermute(left, "cols", [(i, i ^ 2) for i in range(cols)]), left], 1
    )
    def along(step, value):
        route = []
        for chip in range(half):
            for odd_chip in range(2):
                source, target = odd_chip * half + chip, 2 * ((chip + step) % half) + odd_chip
                route += [(2 * source + c, 2 * target + c) for c in range(2)]
        return lax.ppermute(value, "cols", route)

    whole = jnp.zeros((2, half, 2, sub, width), bf16)
    block = along(0, grad)
    for step in range(half):
        if step < half - 1:
            grad, block, left_pair, later = lax.optimization_barrier((grad, block, left_pair, later))
            ahead = along(step + 1, grad)
        other = lax.ppermute(block, "cols", [(i, i ^ 1) for i in range(cols)])
        both = jnp.where(core == 0, jnp.stack([block, other]), jnp.stack([other, block]))
        parts = product(both, left_pair).reshape(2, rows, sub, 2 * width)
        mark = parts
        sums = scatter_sum(parts.swapaxes(0, 1))
        sums = sums.astype(bf16)
        if step == half - 2:
            later, ahead = lax.optimization_barrier((later, ahead))
        if step < half - 1:
            block, _ = lax.optimization_barrier((ahead, sums))
        got = lax.ppermute(sums[..., :width], "cols", [(i, i ^ 2) for i in range(cols)])
        chip = lax.rem(pair + half - step, half)
        for half_index, value in ((odd, sums[..., width:]), (1 - odd, got)):
            whole = lax.dynamic_update_slice(
                whole, value[None, None], (half_index, chip, 0, 0, 0)
            )
    return whole.reshape(depth, width), later, mark


def make_local(rows, cols):
    def local(forget_grad, left_basis, right_basis, first_moment, second_moment):
        depth, width = right_basis.shape
        per = cols // rows
        sub = width // rows
        mid = width // 2
        spans = (slice(0, mid), slice(mid, width))

        dealt = deal(right_basis.reshape(per, rows, sub, width)).reshape(depth, width)
        half, dealt, mark = rotate_left(forget_grad, left_basis, dealt, rows, cols)
        left, half = lax.optimization_barrier((left_basis, half))
        right_rows = lax.all_gather(dealt, "cols", axis=1, tiled=True)
        left_rows = lax.all_gather(left, "cols", axis=1, tiled=True)
        left_rows = left_rows.reshape(depth, cols, 2, mid)

        values = []
        for span in spans:
            parts = lax.dot_general(
                right_rows, half[:, span], (((0,), (0,)), ((), ())), preferred_element_type=f32
            ).astype(bf16)
            values.append(-scatter_sum(rows_first(parts).reshape(rows, depth, mid)))
        rotated = jnp.concatenate(values, 1)

        step_dir = None
        for c, (span, value) in enumerate(zip(spans, values)):
            new_first = beta_first * first_moment[:, span] + (1.0 - beta_first) * value
            new_second = beta_second * second_moment[:, span] + (1.0 - beta_second) * value * value
            normal = new_first / corr_first / (jnp.sqrt(new_second / corr_second) + epsilon)
            normals = gather(normal.astype(bf16), rows).reshape(rows * depth, mid)
            term = jnp.dot(right_rows, normals, preferred_element_type=f32).astype(bf16)
            term = lax.all_to_all(rows_first(term).reshape(cols, sub, mid), "cols", 0, 1)
            term = lax.dot_general(
                left_rows[:, :, c].reshape(depth, cols * mid),
                gather(term.reshape(sub, cols * mid), rows).reshape(width, cols * mid),
                (((1,), (1,)), ((), ())),
                preferred_element_type=f32,
            )
            step_dir = term if step_dir is None else step_dir + term
        step_dir = step_dir.astype(bf16)

        new_first = beta_first * first_moment + (1.0 - beta_first) * rotated
        new_second = beta_second * second_moment + (1.0 - beta_second) * rotated * rotated
        return (step_dir, new_first, new_second)

    return local


def solution(mesh):
    spec = P("rows", "cols")
    return jax.shard_map(
        make_local(mesh.shape["rows"], mesh.shape["cols"]),
        mesh=mesh,
        in_specs=(spec,) * 5,
        out_specs=(spec,) * 3,
        check_vma=False,
    )
```

```python
import jax
import jax.numpy as jnp
from jax import lax
from jax.experimental.layout import Layout, with_layout_constraint
from jax.sharding import PartitionSpec as P

beta_first = 0.9
beta_second = 0.95
corr_first = 1.0 - 0.9**10
corr_second = 1.0 - 0.95**10
epsilon = 1e-08

bf16 = jnp.bfloat16
f32 = jnp.float32
chunks = 2


def rows_first(value):
    return with_layout_constraint(value, Layout(major_to_minor=tuple(range(value.ndim))))


def swap(block, count, mask):
    return lax.ppermute(block, "rows", [(i, i ^ mask) for i in range(count)])


def partners(count):
    return sorted(range(1, count), key=lambda mask: -mask.bit_count())


def halve(parts, reverse):
    count = parts.shape[0]
    me = lax.axis_index("rows")
    bits = list(range(count.bit_length() - 1))
    held = bits[::-1]
    parts = parts.reshape((2,) * len(held) + parts.shape[1:])
    for bit in bits[::-1] if reverse else bits:
        axis = held.index(bit)
        mine = (me >> bit) & 1
        got = swap(lax.dynamic_index_in_dim(parts, 1 - mine, axis, False), count, 1 << bit)
        kept = lax.dynamic_index_in_dim(parts, mine, axis, False)
        held.remove(bit)
        total = kept.astype(f32) + got.astype(f32)
        parts = total.astype(bf16) if held else total
    return parts


def scatter_sum(parts):
    cut = parts.shape[1] // 2
    return jnp.concatenate([halve(parts[:, :cut], False), halve(parts[:, cut:], True)], 0)


def gather(block, count, before=None):
    me = lax.axis_index("rows")
    held = {0: block}
    bits = [1 << b for b in range(count.bit_length() - 1)]
    for bit in bits[:-2]:
        held.update({mask ^ bit: swap(held[mask], count, bit) for mask in list(held)})
    low, high = bits[-2:]
    near = {m ^ b: swap(held[m], count, b) for b in (low, high) for m in list(held)}
    cut = block.shape[0] // 2
    far = {
        m ^ low ^ high: jnp.concatenate(
            [swap(near[m ^ low][:cut], count, high), swap(near[m ^ high][cut:], count, low)], 0
        )
        for m in held
    }
    if before is not None:
        block, before = lax.optimization_barrier((block, before))
    whole = jnp.zeros((count,) + block.shape, block.dtype)
    for mask, term in {**held, **near, **far, 0: block}.items():
        whole = lax.dynamic_update_index_in_dim(whole, term, me ^ mask, 0)
    return whole if before is None else (whole, before)


def deal(parts):
    count = parts.shape[1]
    me = lax.axis_index("rows")
    own = lax.dynamic_index_in_dim(parts, me, 1, False)
    whole = lax.dynamic_update_index_in_dim(jnp.zeros((count,) + own.shape, own.dtype), own, me, 0)
    got = [
        (mask, swap(lax.dynamic_index_in_dim(parts, me ^ mask, 1, False), count, mask))
        for mask in partners(count)
    ]
    for mask, term in got:
        whole = lax.dynamic_update_index_in_dim(whole, term, me ^ mask, 0)
    return whole


def product(blocks, left):
    return lax.dot_general(
        blocks, left, (((1,), (0,)), ((), ())), preferred_element_type=f32
    ).astype(bf16)


def rotate_left(grad, left, later, rows, cols):
    depth, width = grad.shape
    sub = width // rows
    half = cols // 4
    index = lax.axis_index("cols")
    core, odd, pair = index & 1, (index >> 1) & 1, index >> 2
    left_pair = jnp.concatenate(
        [lax.ppermute(left, "cols", [(i, i ^ 2) for i in range(cols)]), left], 1
    )
    def along(step, value):
        route = []
        for chip in range(half):
            for odd_chip in range(2):
                source, target = odd_chip * half + chip, 2 * ((chip + step) % half) + odd_chip
                route += [(2 * source + c, 2 * target + c) for c in range(2)]
        return lax.ppermute(value, "cols", route)

    whole = jnp.zeros((2, half, 2, sub, width), bf16)
    block = along(0, grad)
    for step in range(half):
        if step < half - 1:
            ahead = along(step + 1, grad)
        other = lax.ppermute(block, "cols", [(i, i ^ 1) for i in range(cols)])
        both = jnp.where(core == 0, jnp.stack([block, other]), jnp.stack([other, block]))
        parts = product(both, left_pair).reshape(2, rows, sub, 2 * width)
        sums = scatter_sum(parts.swapaxes(0, 1))
        sums = sums.astype(bf16)
        if step == half - 2:
            later, ahead = lax.optimization_barrier((later, ahead))
        if step < half - 1:
            block, _ = lax.optimization_barrier((ahead, sums))
        got = lax.ppermute(sums[..., :width], "cols", [(i, i ^ 2) for i in range(cols)])
        chip = lax.rem(pair + half - step, half)
        for half_index, value in ((odd, sums[..., width:]), (1 - odd, got)):
            whole = lax.dynamic_update_slice(
                whole, value[None, None], (half_index, chip, 0, 0, 0)
            )
    return whole.reshape(depth, width), later


def make_local(rows, cols):
    def local(forget_grad, left_basis, right_basis, first_moment, second_moment):
        depth, width = right_basis.shape
        per = cols // rows
        sub = width // rows
        mid = width // 2
        spans = (slice(0, mid), slice(mid, width))

        dealt = deal(right_basis.reshape(per, rows, sub, width)).reshape(depth, width)
        half, dealt = rotate_left(forget_grad, left_basis, dealt, rows, cols)
        left, half = lax.optimization_barrier((left_basis, half))
        right_rows = lax.all_gather(dealt, "cols", axis=1, tiled=True)
        left_rows = lax.all_gather(left, "cols", axis=1, tiled=True)
        left_rows = left_rows.reshape(depth, cols, 2, mid)

        parts = [
            rows_first(
                lax.dot_general(
                    right_rows, half[:, span], (((0,), (0,)), ((), ())), preferred_element_type=f32
                ).astype(bf16)
            ).reshape(rows, depth, mid)
            for span in spans
        ]
        value, parts[1] = lax.optimization_barrier((scatter_sum(parts[0]), parts[1]))
        values = [value, scatter_sum(parts[1])]
        values = [-value for value in values]
        rotated = jnp.concatenate(values, 1)

        def finish(term, c):
            term = lax.all_to_all(term.reshape(cols, sub, mid), "cols", 0, 1)
            return lax.dot_general(
                left_rows[:, :, c].reshape(depth, cols * mid),
                gather(term.reshape(sub, cols * mid), rows).reshape(width, cols * mid),
                (((1,), (1,)), ((), ())),
                preferred_element_type=f32,
            )

        step_dir = None
        last = None
        for c, (span, value) in enumerate(zip(spans, values)):
            new_first = beta_first * first_moment[:, span] + (1.0 - beta_first) * value
            new_second = beta_second * second_moment[:, span] + (1.0 - beta_second) * value * value
            normal = new_first / corr_first / (jnp.sqrt(new_second / corr_second) + epsilon)
            if last is None:
                normals = gather(normal.astype(bf16), rows)
            else:
                normals, last = gather(normal.astype(bf16), rows, last)
            normals = normals.reshape(rows * depth, mid)
            if last is not None:
                step_dir = finish(last, 0)
            term = jnp.dot(right_rows, normals, preferred_element_type=f32).astype(bf16)
            last = rows_first(term)
        step_dir = (step_dir + finish(last, 1))
        step_dir = step_dir.astype(bf16)

        new_first = beta_first * first_moment + (1.0 - beta_first) * rotated
        new_second = beta_second * second_moment + (1.0 - beta_second) * rotated * rotated
        return (step_dir, new_first, new_second)

    return local


def solution(mesh):
    spec = P("rows", "cols")
    return jax.shard_map(
        make_local(mesh.shape["rows"], mesh.shape["cols"]),
        mesh=mesh,
        in_specs=(spec,) * 5,
        out_specs=(spec,) * 3,
        check_vma=False,
    )
```

```python
import jax
import jax.numpy as jnp
from jax import lax
from jax.experimental.layout import Layout, with_layout_constraint
from jax.sharding import PartitionSpec as P

beta_first = 0.9
beta_second = 0.95
corr_first = 1.0 - 0.9**10
corr_second = 1.0 - 0.95**10
epsilon = 1e-08

bf16 = jnp.bfloat16
f32 = jnp.float32
chunks = 2


def rows_first(value):
    return with_layout_constraint(value, Layout(major_to_minor=tuple(range(value.ndim))))


def swap(block, count, mask):
    return lax.ppermute(block, "rows", [(i, i ^ mask) for i in range(count)])


def partners(count):
    return sorted(range(1, count), key=lambda mask: -mask.bit_count())


def halve(parts, reverse):
    count = parts.shape[0]
    me = lax.axis_index("rows")
    bits = list(range(count.bit_length() - 1))
    held = bits[::-1]
    parts = parts.reshape((2,) * len(held) + parts.shape[1:])
    for bit in bits[::-1] if reverse else bits:
        axis = held.index(bit)
        mine = (me >> bit) & 1
        got = swap(lax.dynamic_index_in_dim(parts, 1 - mine, axis, False), count, 1 << bit)
        kept = lax.dynamic_index_in_dim(parts, mine, axis, False)
        held.remove(bit)
        total = kept.astype(f32) + got.astype(f32)
        parts = total.astype(bf16) if held else total
    return parts


def scatter_sum(parts):
    cut = parts.shape[1] // 2
    return jnp.concatenate([halve(parts[:, :cut], False), halve(parts[:, cut:], True)], 0)


def gather(block, count, before=None):
    me = lax.axis_index("rows")
    held = {0: block}
    bits = [1 << b for b in range(count.bit_length() - 1)]
    for bit in bits[:-2]:
        held.update({mask ^ bit: swap(held[mask], count, bit) for mask in list(held)})
    low, high = bits[-2:]
    near = {m ^ b: swap(held[m], count, b) for b in (low, high) for m in list(held)}
    cut = block.shape[0] // 2
    far = {
        m ^ low ^ high: jnp.concatenate(
            [swap(near[m ^ low][:cut], count, high), swap(near[m ^ high][cut:], count, low)], 0
        )
        for m in held
    }
    if before is not None:
        block, before = lax.optimization_barrier((block, before))
    whole = jnp.zeros((count,) + block.shape, block.dtype)
    for mask, term in {**held, **near, **far, 0: block}.items():
        whole = lax.dynamic_update_index_in_dim(whole, term, me ^ mask, 0)
    return whole if before is None else (whole, before)


def deal(parts):
    count = parts.shape[1]
    me = lax.axis_index("rows")
    own = lax.dynamic_index_in_dim(parts, me, 1, False)
    whole = lax.dynamic_update_index_in_dim(jnp.zeros((count,) + own.shape, own.dtype), own, me, 0)
    got = [
        (mask, swap(lax.dynamic_index_in_dim(parts, me ^ mask, 1, False), count, mask))
        for mask in partners(count)
    ]
    for mask, term in got:
        whole = lax.dynamic_update_index_in_dim(whole, term, me ^ mask, 0)
    return whole


def product(blocks, left):
    return lax.dot_general(
        blocks, left, (((1,), (0,)), ((), ())), preferred_element_type=f32
    ).astype(bf16)


def rotate_left(grad, left, later, rows, cols):
    depth, width = grad.shape
    sub = width // rows
    half = cols // 4
    index = lax.axis_index("cols")
    core, odd, pair = index & 1, (index >> 1) & 1, index >> 2
    left_pair = jnp.concatenate(
        [lax.ppermute(left, "cols", [(i, i ^ 2) for i in range(cols)]), left], 1
    )
    def along(step, value):
        route = []
        for chip in range(half):
            for odd_chip in range(2):
                source, target = odd_chip * half + chip, 2 * ((chip + step) % half) + odd_chip
                route += [(2 * source + c, 2 * target + c) for c in range(2)]
        return lax.ppermute(value, "cols", route)

    whole = jnp.zeros((2, half, 2, sub, width), bf16)
    block = along(0, grad)
    for step in range(half):
        if step < half - 1:
            ahead = along(step + 1, grad)
        other = lax.ppermute(block, "cols", [(i, i ^ 1) for i in range(cols)])
        both = jnp.where(core == 0, jnp.stack([block, other]), jnp.stack([other, block]))
        parts = product(both, left_pair).reshape(2, rows, sub, 2 * width)
        sums = scatter_sum(parts.swapaxes(0, 1))
        sums = sums.astype(bf16)
        if step == half - 2:
            later, ahead = lax.optimization_barrier((later, ahead))
        if step < half - 1:
            block, _ = lax.optimization_barrier((ahead, sums))
        got = lax.ppermute(sums[..., :width], "cols", [(i, i ^ 2) for i in range(cols)])
        chip = lax.rem(pair + half - step, half)
        for half_index, value in ((odd, sums[..., width:]), (1 - odd, got)):
            whole = lax.dynamic_update_slice(
                whole, value[None, None], (half_index, chip, 0, 0, 0)
            )
    return whole.reshape(depth, width), later


def make_local(rows, cols):
    def local(forget_grad, left_basis, right_basis, first_moment, second_moment):
        depth, width = right_basis.shape
        per = cols // rows
        sub = width // rows
        mid = width // 2
        spans = (slice(0, mid), slice(mid, width))

        dealt = deal(right_basis.reshape(per, rows, sub, width)).reshape(depth, width)
        half, dealt = rotate_left(forget_grad, left_basis, dealt, rows, cols)
        left, half = lax.optimization_barrier((left_basis, half))
        right_rows = lax.all_gather(dealt, "cols", axis=1, tiled=True)
        left_rows = lax.all_gather(left, "cols", axis=1, tiled=True)
        left_rows = left_rows.reshape(depth, cols, 2, mid)

        parts = [
            rows_first(
                lax.dot_general(
                    right_rows, half[:, span], (((0,), (0,)), ((), ())), preferred_element_type=f32
                ).astype(bf16)
            ).reshape(rows, depth, mid)
            for span in spans
        ]
        value, parts[1] = lax.optimization_barrier((scatter_sum(parts[0]), parts[1]))
        values = [value, scatter_sum(parts[1])]
        values = [-value for value in values]
        rotated = jnp.concatenate(values, 1)

        def finish(term, c, before=None):
            term = lax.all_to_all(term.reshape(cols, sub, mid), "cols", 0, 1)
            whole = gather(term.reshape(sub, cols * mid), rows, before)
            if before is not None:
                whole, before = whole
            product = lax.dot_general(
                left_rows[:, :, c].reshape(depth, cols * mid),
                whole.reshape(width, cols * mid),
                (((1,), (1,)), ((), ())),
                preferred_element_type=f32,
            )
            return product if before is None else before + product

        step_dir = None
        last = None
        for c, (span, value) in enumerate(zip(spans, values)):
            new_first = beta_first * first_moment[:, span] + (1.0 - beta_first) * value
            new_second = beta_second * second_moment[:, span] + (1.0 - beta_second) * value * value
            normal = new_first / corr_first / (jnp.sqrt(new_second / corr_second) + epsilon)
            if last is None:
                normals = gather(normal.astype(bf16), rows)
            else:
                normals, last = gather(normal.astype(bf16), rows, last)
            normals = normals.reshape(rows * depth, mid)
            if last is not None:
                step_dir = finish(last, 0)
            term = jnp.dot(right_rows, normals, preferred_element_type=f32).astype(bf16)
            last = rows_first(term)
        step_dir = finish(last, 1, step_dir)
        step_dir = step_dir.astype(bf16)

        new_first = beta_first * first_moment + (1.0 - beta_first) * rotated
        new_second = beta_second * second_moment + (1.0 - beta_second) * rotated * rotated
        return (step_dir, new_first, new_second)

    return local


def solution(mesh):
    spec = P("rows", "cols")
    return jax.shard_map(
        make_local(mesh.shape["rows"], mesh.shape["cols"]),
        mesh=mesh,
        in_specs=(spec,) * 5,
        out_specs=(spec,) * 3,
        check_vma=False,
    )
```

```python
import jax
import jax.numpy as jnp
from jax import lax
from jax.experimental.layout import Layout, with_layout_constraint
from jax.sharding import PartitionSpec as P

beta_first = 0.9
beta_second = 0.95
corr_first = 1.0 - 0.9**10
corr_second = 1.0 - 0.95**10
epsilon = 1e-08

bf16 = jnp.bfloat16
f32 = jnp.float32
chunks = 2


def rows_first(value):
    return with_layout_constraint(value, Layout(major_to_minor=tuple(range(value.ndim))))


def swap(block, count, mask):
    return lax.ppermute(block, "rows", [(i, i ^ mask) for i in range(count)])


def partners(count):
    return sorted(range(1, count), key=lambda mask: -mask.bit_count())


def halve(parts, reverse):
    count = parts.shape[0]
    me = lax.axis_index("rows")
    bits = list(range(count.bit_length() - 1))
    held = bits[::-1]
    parts = parts.reshape((2,) * len(held) + parts.shape[1:])
    for bit in bits[::-1] if reverse else bits:
        axis = held.index(bit)
        mine = (me >> bit) & 1
        got = swap(lax.dynamic_index_in_dim(parts, 1 - mine, axis, False), count, 1 << bit)
        kept = lax.dynamic_index_in_dim(parts, mine, axis, False)
        held.remove(bit)
        total = kept.astype(f32) + got.astype(f32)
        parts = total.astype(bf16) if held else total
    return parts


def scatter_sum(parts):
    cut = parts.shape[1] // 2
    return jnp.concatenate([halve(parts[:, :cut], False), halve(parts[:, cut:], True)], 0)


def gather(block, count, before=None):
    me = lax.axis_index("rows")
    held = {0: block}
    bits = [1 << b for b in range(count.bit_length() - 1)]
    for bit in bits[:-2]:
        held.update({mask ^ bit: swap(held[mask], count, bit) for mask in list(held)})
    low, high = bits[-2:]
    near = {m ^ b: swap(held[m], count, b) for b in (low, high) for m in list(held)}
    cut = block.shape[0] // 2
    far = {
        m ^ low ^ high: jnp.concatenate(
            [swap(near[m ^ low][:cut], count, high), swap(near[m ^ high][cut:], count, low)], 0
        )
        for m in held
    }
    if before is not None:
        block, before = lax.optimization_barrier((block, before))
    whole = jnp.zeros((count,) + block.shape, block.dtype)
    for mask, term in {**held, **near, **far, 0: block}.items():
        whole = lax.dynamic_update_index_in_dim(whole, term, me ^ mask, 0)
    return whole if before is None else (whole, before)


def deal(parts):
    count = parts.shape[1]
    me = lax.axis_index("rows")
    own = lax.dynamic_index_in_dim(parts, me, 1, False)
    whole = lax.dynamic_update_index_in_dim(jnp.zeros((count,) + own.shape, own.dtype), own, me, 0)
    got = [
        (mask, swap(lax.dynamic_index_in_dim(parts, me ^ mask, 1, False), count, mask))
        for mask in partners(count)
    ]
    for mask, term in got:
        whole = lax.dynamic_update_index_in_dim(whole, term, me ^ mask, 0)
    return whole


def product(blocks, left):
    return lax.dot_general(
        blocks, left, (((1,), (0,)), ((), ())), preferred_element_type=f32
    ).astype(bf16)


def rotate_left(grad, left, later, rows, cols):
    depth, width = grad.shape
    sub = width // rows
    half = cols // 4
    index = lax.axis_index("cols")
    core, odd, pair = index & 1, (index >> 1) & 1, index >> 2
    left_pair = jnp.concatenate(
        [lax.ppermute(left, "cols", [(i, i ^ 2) for i in range(cols)]), left], 1
    )
    def along(step, value):
        route = []
        for chip in range(half):
            for odd_chip in range(2):
                source, target = odd_chip * half + chip, 2 * ((chip + step) % half) + odd_chip
                route += [(2 * source + c, 2 * target + c) for c in range(2)]
        return lax.ppermute(value, "cols", route)

    whole = jnp.zeros((2, half, 2, sub, width), bf16)
    block = along(0, grad)
    for step in range(half):
        if step < half - 1:
            ahead = along(step + 1, grad)
        other = lax.ppermute(block, "cols", [(i, i ^ 1) for i in range(cols)])
        both = jnp.where(core == 0, jnp.stack([block, other]), jnp.stack([other, block]))
        parts = product(both, left_pair).reshape(2, rows, sub, 2 * width)
        sums = scatter_sum(parts.swapaxes(0, 1))
        sums = sums.astype(bf16)
        if step == half - 2:
            later, ahead = lax.optimization_barrier((later, ahead))
        if step < half - 1:
            block, _ = lax.optimization_barrier((ahead, sums))
        got = lax.ppermute(sums[..., :width], "cols", [(i, i ^ 2) for i in range(cols)])
        chip = lax.rem(pair + half - step, half)
        for half_index, value in ((odd, sums[..., width:]), (1 - odd, got)):
            whole = lax.dynamic_update_slice(
                whole, value[None, None], (half_index, chip, 0, 0, 0)
            )
    return whole.reshape(depth, width), later


def make_local(rows, cols):
    def local(forget_grad, left_basis, right_basis, first_moment, second_moment):
        depth, width = right_basis.shape
        per = cols // rows
        sub = width // rows
        mid = width // 2
        spans = (slice(mid, width), slice(0, mid))

        dealt = deal(right_basis.reshape(per, rows, sub, width)).reshape(depth, width)
        half, dealt = rotate_left(forget_grad, left_basis, dealt, rows, cols)
        left, half = lax.optimization_barrier((left_basis, half))
        right_rows = lax.all_gather(dealt, "cols", axis=1, tiled=True)
        left_rows = lax.all_gather(left, "cols", axis=1, tiled=True)
        left_rows = left_rows.reshape(depth, cols, 2, mid)

        parts = [
            rows_first(
                lax.dot_general(
                    right_rows, half[:, span], (((0,), (0,)), ((), ())), preferred_element_type=f32
                ).astype(bf16)
            ).reshape(rows, depth, mid)
            for span in spans
        ]
        value, parts[1] = lax.optimization_barrier((scatter_sum(parts[0]), parts[1]))
        values = [value, scatter_sum(parts[1])]
        values = [-value for value in values]
        rotated = jnp.concatenate(values[::-1], 1)

        def finish(term, c):
            term = lax.all_to_all(term.reshape(cols, sub, mid), "cols", 0, 1)
            return lax.dot_general(
                left_rows[:, :, 1 - c].reshape(depth, cols * mid),
                gather(term.reshape(sub, cols * mid), rows).reshape(width, cols * mid),
                (((1,), (1,)), ((), ())),
                preferred_element_type=f32,
            )

        step_dir = None
        last = None
        for c, (span, value) in enumerate(zip(spans, values)):
            new_first = beta_first * first_moment[:, span] + (1.0 - beta_first) * value
            new_second = beta_second * second_moment[:, span] + (1.0 - beta_second) * value * value
            normal = new_first / corr_first / (jnp.sqrt(new_second / corr_second) + epsilon)
            if last is None:
                normals = gather(normal.astype(bf16), rows)
            else:
                normals, last = gather(normal.astype(bf16), rows, last)
            normals = normals.reshape(rows * depth, mid)
            if last is not None:
                step_dir = finish(last, 0)
            term = jnp.dot(right_rows, normals, preferred_element_type=f32).astype(bf16)
            last = rows_first(term)
        step_dir = (step_dir + finish(last, 1))
        step_dir = step_dir.astype(bf16)

        new_first = beta_first * first_moment + (1.0 - beta_first) * rotated
        new_second = beta_second * second_moment + (1.0 - beta_second) * rotated * rotated
        return (step_dir, new_first, new_second)

    return local


def solution(mesh):
    spec = P("rows", "cols")
    return jax.shard_map(
        make_local(mesh.shape["rows"], mesh.shape["cols"]),
        mesh=mesh,
        in_specs=(spec,) * 5,
        out_specs=(spec,) * 3,
        check_vma=False,
    )
```
